32 devices in a mesh: ia: 8 (over z, x), ja: 2 (over y), row: 2 (over core).
Axes of the slice: x: 2, y: 2, z: 4, core: 2. Of those that a mesh axis runs over, the one named last changes fastest.
Arguments:
- amplitudes: float32 [16, 16, 1024, 1024], P('ia', ('ja', 'row')), may hold values from -6 to 6
- cycle_inter: float32 [2, 16, 1024, 1024], P(None, ('ja', 'row'), 'ia'), may hold values from -0.125 to 0.125
- occ_energy: float32 [256], replicated, may hold values from -2 to -0.3
- virt_energy: float32 [1024], replicated, may hold values from 0.3 to 3
- window_orbs: int32 [16], replicated, may hold values from 0 to 255, as said below
- internal_pos: int32 [2], replicated, may hold values from 0 to 15, as said below
- virt_order: int32 [1024], replicated, may hold values from 0 to 1023, each once
Outputs:
- updated: float32 [16, 16, 1024, 1024], P('ia', ('ja', 'row'))
The draws below stay inside these ranges and needn't reach their ends.
Inputs may be any that keep to these rules, and one draw needn't show every extreme that they name: `window_orbs`: 16 distinct orbital numbers. `internal_pos`: 2 distinct window positions, one of which is the last position 15.
All inputs are finite; a program needn't handle non-finite values.
Results may differ from the reference program's by a relative error of at most 0.00005.
Values sent between devices are 32-bit elements; how exact they have to be, the bound alone decides.
A program may use at most 192 MiB of HBM per device.

```python
import jax
import jax.numpy as jnp
from jax import lax

V = 1024
NOCC = 256
NW = 16
NK = 2


def draw_window_orbs(key, part):
    return jax.random.permutation(jax.random.fold_in(key, 11), NOCC)[:NW].astype(jnp.int32)


def draw_internal_pos(key, part):
    others = jax.random.permutation(jax.random.fold_in(key, 12), NW - 1)[:NK - 1].astype(jnp.int32)
    joined = jnp.concatenate([others, jnp.full((1,), NW - 1, dtype=jnp.int32)])
    order = jax.random.permutation(jax.random.fold_in(key, 13), NK).astype(jnp.int32)
    return jnp.take(joined, order).astype(jnp.int32)


def shard_levels(rng, dims, cuts, low, top_value):
    level, own = 1.0, jax.random.fold_in(rng, 6)
    for axis_at, blocks in cuts:
        draws = jnp.exp(jax.random.uniform(jax.random.fold_in(own, axis_at), (blocks,), jnp.float32, low / len(cuts), top_value / len(cuts)))
        level = level * jnp.repeat(draws, dims[axis_at] // blocks).reshape([-1 if axis == axis_at else 1 for axis in range(len(dims))])
    return level


def normal_values(own_key, dims, width, bound, cuts=(), held_as=jnp.bfloat16):
    level = shard_levels(own_key, dims, cuts, -0.22, 0.18) if cuts else 1.0
    result = jax.random.normal(own_key, dims, jnp.float32) * width * level
    return jnp.minimum(jnp.maximum(result, -bound), bound).astype(held_as)


def setup_inputs(seed: int = 0) -> dict:
    keys = jax.random.split(jax.random.key(seed), 8)
    return {
        "amplitudes": normal_values(keys[0], (NW, NW, V, V), 1.0, 6.0, ((0, 8), (1, 4)), jnp.float32),
        "cycle_inter": normal_values(keys[1], (NK, NW, V, V), (NK * V) ** -0.5, 0.125, ((1, 4), (2, 8)), jnp.float32),
        "occ_energy": jnp.clip(jax.random.uniform(keys[2], (NOCC,), jnp.float32, -2.0, -0.3), -2.0, -0.3),
        "virt_energy": jnp.clip(jax.random.uniform(keys[3], (V,), jnp.float32, 0.3, 3.0), 0.3, 3.0),
        "window_orbs": draw_window_orbs(jax.random.fold_in(keys[7], 71), 0),
        "internal_pos": draw_internal_pos(jax.random.fold_in(keys[7], 71), 0),
        "virt_order": jax.random.permutation(keys[6], V).astype(jnp.int32),
    }


def reference(amplitudes, cycle_inter, occ_energy, virt_energy, window_orbs, internal_pos, virt_order):
    hits = window_orbs[:, None] == jnp.arange(NOCC, dtype=jnp.int32)[None, :]
    e_window = jnp.sum(jnp.where(hits, occ_energy[None, :], 0.0), axis=1)
    e_virt = jnp.take(virt_energy, virt_order)
    chosen = jnp.take(amplitudes, internal_pos, axis=1)
    pair_x = 2.0 * chosen - jnp.swapaxes(chosen, 2, 3)
    cycle = jnp.einsum("ikac,kjcb->ijab", pair_x, cycle_inter, precision=lax.Precision.HIGHEST)

    def one_row(index):
        own = lax.dynamic_index_in_dim(cycle, index, 0, keepdims=False)
        mirrored = jnp.swapaxes(lax.dynamic_index_in_dim(cycle, index, 1, keepdims=False), 1, 2)
        before = lax.dynamic_index_in_dim(amplitudes, index, 0, keepdims=False)
        e_first = lax.dynamic_index_in_dim(e_window, index, 0, keepdims=False)
        denom = ((e_first + e_window[:, None, None]) - e_virt[None, :, None]) - e_virt[None, None, :]
        return before + (own + mirrored) / denom

    return lax.map(one_row, jnp.arange(NW, dtype=jnp.int32))
```

```python
import functools

import jax
import jax.numpy as jnp
from jax import lax
from jax.experimental import pallas as pl
from jax.experimental.pallas import tpu as pltpu
from jax.sharding import PartitionSpec as P

COLS = ("ja", "row")
ALL = ("ia", "ja", "row")


def mirror(blocks_for, ia_size, jr_size):
    k = ia_size // jr_size
    sub = lax.rem(lax.axis_index("ia"), k)
    got = []
    for turn in range(k):
        pairs = []
        for a in range(jr_size):
            for s in range(k):
                for b in range(jr_size):
                    t = (turn - s) % k
                    pairs.append(((k * a + s) * jr_size + b, (k * b + t) * jr_size + a))
        other = lax.rem(turn - sub + k, k)
        got.append((other, lax.ppermute(blocks_for(other), ALL, pairs)))
    return got


def ring_gather(piece, ia_size, depth):
    lead = piece.shape[:2]
    width = piece.shape[3]
    me = lax.axis_index("ia")
    swap = [(d, d ^ 1) for d in range(ia_size)]
    step = [(d, (d + 2) % ia_size) for d in range(ia_size)]
    full = jnp.zeros(lead + (ia_size * depth, width), piece.dtype)
    marks = []
    for s in range(ia_size // 2):
        owner = lax.rem(me - 2 * s + ia_size, ia_size)
        partner = lax.ppermute(piece, "ia", swap)
        marks.append(partner)
        following = lax.ppermute(piece, "ia", step) if s < ia_size // 2 - 1 else None
        full = lax.dynamic_update_slice_in_dim(full, piece, owner * depth, 2)
        full = lax.dynamic_update_slice_in_dim(full, partner, (owner ^ 1) * depth, 2)
        piece = following
    return full, marks


def split(value):
    high = value.astype(jnp.bfloat16)
    return high, (value - high.astype(jnp.float32)).astype(jnp.bfloat16)


def form_rows(amplitudes, internal_pos):
    tile_rows, tile_cols, virt, _ = amplitudes.shape
    count_k = internal_pos.shape[0]
    band = 256 if virt % 256 == 0 else virt

    def body(at_col, where, local, amp_ref, out_ref):
        mine = where[pl.program_id(0)] == at_col[0]
        for at in range(virt // band):
            rows = slice(at * band, (at + 1) * band)
            formed = 2.0 * amp_ref[0, 0, rows, :] - amp_ref[0, 0, :, rows].T
            out_ref[0, 0, rows, :] = jnp.where(mine, formed, 0.0)

    return pl.pallas_call(
        body,
        grid_spec=pltpu.PrefetchScalarGridSpec(
            num_scalar_prefetch=3,
            grid=(count_k, tile_rows),
            in_specs=[
                pl.BlockSpec((1, 1, virt, virt), lambda m, i, c, w, local: (i, local[m], 0, 0))
            ],
            out_specs=pl.BlockSpec((1, 1, virt, virt), lambda m, i, c, w, local: (m, i, 0, 0)),
        ),
        out_shape=jax.ShapeDtypeStruct((count_k, tile_rows, virt, virt), jnp.float32),
        compiler_params=pltpu.CompilerParams(vmem_limit_bytes=40 * 1024 * 1024),
        name="form_rows",
    )(
        lax.axis_index(COLS).astype(jnp.int32)[None],
        internal_pos // tile_cols,
        internal_pos % tile_cols,
        amplitudes,
    )


def turned(x_rows, which, depth):
    count_k, tile_rows, virt, _ = x_rows.shape
    if depth % 128:
        block = lax.dynamic_slice_in_dim(x_rows, which * depth, depth, 3)
        return jnp.swapaxes(block, 2, 3)

    def body(at, x_ref, out_ref):
        out_ref[0, 0] = x_ref[0, 0].T

    return pl.pallas_call(
        body,
        grid_spec=pltpu.PrefetchScalarGridSpec(
            num_scalar_prefetch=1,
            grid=(count_k, tile_rows),
            in_specs=[pl.BlockSpec((1, 1, virt, depth), lambda m, i, at: (m, i, 0, at[0]))],
            out_specs=pl.BlockSpec((1, 1, depth, virt), lambda m, i, at: (m, i, 0, 0)),
        ),
        out_shape=jax.ShapeDtypeStruct((count_k, tile_rows, depth, virt), jnp.float32),
        compiler_params=pltpu.CompilerParams(vmem_limit_bytes=52 * 1024 * 1024),
        name="turned",
    )(which.astype(jnp.int32)[None], x_rows)


def product_kernel(col, band, last, left_ref, right_ref, *rest):
    out_ref, total, high, low = rest[-4:]
    row, block = pl.program_id(0), pl.program_id(1)
    count_k, depth = right_ref.shape[0], right_ref.shape[2]
    for m in range(count_k):
        rows = pl.ds(m * depth, depth)
        high[rows, :], low[rows, :] = split(right_ref[m, 0])

    @pl.when(block == 0)
    def _():
        total[...] = jnp.zeros_like(total)

    def one_band(at, carry):
        rows = pl.ds(pl.multiple_of(at * band, band), band)
        left = jnp.concatenate([left_ref[m, 0, rows, :] for m in range(count_k)], axis=1)
        left_high, left_low = split(left)
        dot = functools.partial(jnp.dot, preferred_element_type=jnp.float32)
        total[rows, :] += (
            dot(left_high, high[...]) + dot(left_high, low[...]) + dot(left_low, high[...])
        )
        return carry

    bands = total.shape[0] // band
    lax.fori_loop(0, bands, one_band, 0)

    @pl.when(block == pl.num_programs(1) - 1)
    def _():
        if not last:
            out_ref[0, 0] = total[...]
            return
        held_ref, e_rows, e_cols, amp_ref, va_ref, vb_ref = rest[:6]
        pair = e_rows[row] + e_cols[col]

        def finish(at, carry):
            rows = pl.ds(pl.multiple_of(at * band, band), band)
            denom = (pair - va_ref[rows, :]) - vb_ref[...]
            both = held_ref[0, 0, rows, :] + total[rows, :]
            out_ref[0, 0, rows, :] = amp_ref[0, 0, rows, :] + both / denom
            return carry

        lax.fori_loop(0, bands, finish, 0)


def product(col, at, left, right, out, shape, energies=None):
    count_k, tile_rows, virt, _ = left.shape
    depth = 256 if virt % 256 == 0 else virt
    band = 256 if virt % 256 == 0 else virt
    tile = pl.BlockSpec((1, 1, virt, virt), lambda i, q: (i, col, 0, 0))
    in_specs = [
        pl.BlockSpec((count_k, 1, virt, depth), lambda i, q: (0, i, 0, q)),
        pl.BlockSpec((count_k, 1, depth, virt), lambda i, q: (0, at, q, 0)),
    ]
    operands = [left, right]
    aliases = {}
    if out is not None:
        aliases = {2: 0}
        in_specs.append(pl.BlockSpec(memory_space=pl.ANY) if energies is None else tile)
        operands.append(out)
    if energies is not None:
        e_rows, e_cols, amplitudes, e_virt = energies
        scalars = pl.BlockSpec(memory_space=pltpu.SMEM)
        in_specs += [
            scalars, scalars, tile,
            pl.BlockSpec((virt, 1), lambda i, q: (0, 0)),
            pl.BlockSpec((1, virt), lambda i, q: (0, 0)),
        ]
        operands += [e_rows, e_cols, amplitudes, e_virt[:, None], e_virt[None]]
    return pl.pallas_call(
        functools.partial(product_kernel, col, band, energies is not None),
        grid=(tile_rows, virt // depth),
        in_specs=in_specs,
        out_specs=tile,
        out_shape=jax.ShapeDtypeStruct(shape, jnp.float32),
        scratch_shapes=[
            pltpu.VMEM((virt, virt), jnp.float32),
            pltpu.VMEM((count_k * depth, virt), jnp.bfloat16),
            pltpu.VMEM((count_k * depth, virt), jnp.bfloat16),
        ],
        input_output_aliases=aliases,
        compiler_params=pltpu.CompilerParams(vmem_limit_bytes=52 * 1024 * 1024),
        cost_estimate=pl.CostEstimate(
            flops=6 * tile_rows * count_k * virt**3,
            bytes_accessed=10 * tile_rows * virt * virt * 4,
            transcendentals=0,
        ),
        name="product" if energies is None else "finish",
    )(*operands)


def on_device(
    amplitudes, cycle_inter, occ_energy, virt_energy, window_orbs, internal_pos, virt_order
):
    tile_rows, tile_cols = amplitudes.shape[:2]
    virt = amplitudes.shape[2]
    count_k = cycle_inter.shape[0]
    depth = cycle_inter.shape[2]
    ia_size = lax.axis_size("ia")
    jr_size = lax.axis_size("ja") * lax.axis_size("row")
    at_col = lax.axis_index(COLS)
    parts = 2 if tile_cols % 2 == 0 else 1
    share = tile_cols // parts

    w_cols, marks = [], []
    for h in range(parts):
        full, partners = ring_gather(cycle_inter[:, h * share : (h + 1) * share], ia_size, depth)
        w_cols.append(full)
        marks.append(partners[max(len(partners) - 2, 0)])

    k = ia_size // jr_size
    w_blocks = mirror(
        lambda t: lax.dynamic_slice_in_dim(cycle_inter, t * tile_rows, tile_rows, 1),
        ia_size,
        jr_size,
    )

    x_rows = lax.psum(form_rows(amplitudes, internal_pos), COLS)
    after = sum(jnp.isnan(mark[0, 0, 0, 0]).astype(jnp.int32) for mark in marks)

    chunk = jnp.zeros((count_k, tile_cols, depth, virt), jnp.float32)
    for s, block in mirror(
        lambda t: turned(x_rows, at_col * k + t + after, depth),
        ia_size,
        jr_size,
    ):
        chunk = lax.dynamic_update_slice_in_dim(chunk, block, s * tile_rows, 1)
    hits = window_orbs[:, None] == jnp.arange(occ_energy.shape[0], dtype=jnp.int32)[None, :]
    e_window = jnp.sum(jnp.where(hits, occ_energy[None, :], 0.0), axis=1)
    e_virt = jnp.take(virt_energy, virt_order)
    e_rows = lax.dynamic_slice_in_dim(e_window, lax.axis_index("ia") * tile_rows, tile_rows)
    e_cols = lax.dynamic_slice_in_dim(e_window, at_col * tile_cols, tile_cols)
    out = None
    for col in range(tile_cols):
        out = product(col, col % share, x_rows, w_cols[col // share], out, amplitudes.shape)
    energies = (e_rows, e_cols, amplitudes, e_virt)
    done = jnp.isnan(out[0, 0, 0, 0]).astype(jnp.int32)
    quarter = jnp.zeros((count_k, tile_rows, k * depth, virt), jnp.float32)
    for s, block in w_blocks:
        quarter = lax.dynamic_update_slice_in_dim(quarter, block, s * depth + done, 2)
    wt_rows = jnp.swapaxes(lax.all_gather(quarter, COLS, axis=2, tiled=True), 2, 3)
    for h in range(parts):
        piece = lax.dynamic_slice_in_dim(chunk, h * share + (done if h else 0), share, 1)
        x_cols = ring_gather(piece, ia_size, depth)[0]
        for at in range(share):
            out = product(h * share + at, at, wt_rows, x_cols, out, amplitudes.shape, energies)
    return out


def solution(mesh):
    placed = (
        P("ia", COLS, None, None),
        P(None, COLS, "ia", None),
        P(),
        P(),
        P(),
        P(),
        P(),
    )
    return jax.shard_map(
        on_device,
        mesh=mesh,
        in_specs=placed,
        out_specs=P("ia", COLS, None, None),
        check_vma=False,
    )
```
